256 devices in a mesh: store: 8 (over z_lo, core), ctx: 32 (over z_hi, y, x).
Axes of the slice: x: 4, y: 4, z: 8 (z_hi: 2, z_lo: 4; z = z_hi * 4 + z_lo), core: 2. Of those that a mesh axis runs over, the one named last changes fastest.
Arguments:
- queries: bfloat16 [4096, 7168], P('ctx', 'store'), may hold values from -10 to 10
- suffix_kv: bfloat16 [4096, 2048], P('ctx', 'store'), may hold values from -6 to 6
- cache: bfloat16 [8, 16, 128, 2048], P('store', None, 'ctx'), may hold values from -10 to 10
- block_list: int32 [8, 8], P('store'), may hold values from 0 to 15, as said below
- counts: int32 [8], replicated, may hold values from 2 to 8, as said below
- out_weight: bfloat16 [7168, 7168], P('store', 'ctx'), may hold values from -2.390625 to 2.390625
- residual: bfloat16 [4096, 7168], P('store', 'ctx'), may hold values from -6 to 6
- norm_gain: bfloat16 [7168], P('ctx'), may hold values from 0.099609375 to 1.8984375
- gate_weight: bfloat16 [7168, 10240], P(None, 'ctx'), may hold values from -0.0625 to 0.0625
- up_weight: bfloat16 [7168, 10240], P(None, 'ctx'), may hold values from -0.0625 to 0.0625
Outputs:
- hidden_state: bfloat16 [4096, 7168], P('store', 'ctx')
- swiglu: bfloat16 [4096, 10240], P('store', 'ctx')
The draws below stay inside these ranges and needn't reach their ends.
Inputs may be any that keep to these rules, and one draw needn't show every extreme that they name: `block_list`: the first counts[g] entries of row g are distinct slots of storage group g holding the prefix's blocks; a row's entries are distinct. `counts`: 32 blocks in all; some group holds exactly 8.
All inputs are finite; a program needn't handle non-finite values.
Results may differ from the reference program's by a relative error of at most 0.029.
Values may be sent and summed in bfloat16 or wider, within the bound.
No kernel may reach another device: no remote copies, remote signals or barrier semaphores. Data moves between devices by JAX's collectives and lax.ppermute only.
A program may use at most 128 MiB of HBM per device.

```python
import jax
import jax.numpy as jnp
from jax import lax

D = 7168
HQ = 56
KVH = 8
HD = 128
FF = 10240
BLK = 128
CAP = 8
GQ = 7
SLOTS = 16
SUFFIX = 4096
N_STORE = 8


def holder_lists(key):
    base_key = jax.random.fold_in(key, 101)
    pattern = jnp.array([CAP, CAP // 4, CAP // 2, CAP // 4], dtype=jnp.int32)
    ordered = pattern[jnp.arange(N_STORE, dtype=jnp.int32) % 4]
    shuffle = jax.random.permutation(jax.random.fold_in(base_key, 1), N_STORE)
    counts = ordered[shuffle]
    group_keys = jax.random.split(jax.random.fold_in(base_key, 2), N_STORE)
    slot_lists = jax.vmap(lambda group_key: jax.random.permutation(group_key, SLOTS)[:CAP])(group_keys)
    return (counts.astype(jnp.int32), slot_lists.astype(jnp.int32))


def draw_counts(key, part):
    counts, slot_lists = holder_lists(key)
    return counts


def draw_block_list(key, part):
    counts, slot_lists = holder_lists(key)
    return slot_lists


def draw_queries(key, part):
    key = jax.random.fold_in(key, 3)
    values = jax.random.truncated_normal(key, -4.0, 4.0, (SUFFIX, HQ * HD), jnp.float32)
    return values.astype(jnp.bfloat16)


def draw_cache(key, part):
    key = jax.random.fold_in(key, 4)
    values = jax.random.truncated_normal(key, -4.0, 4.0, (N_STORE, SLOTS, BLK, KVH * 2 * HD), jnp.float32)
    return values.astype(jnp.bfloat16)


def draw_residual(key, part):
    key = jax.random.fold_in(key, 5)
    position = jnp.arange(D, dtype=jnp.float32) / D
    values = jax.random.truncated_normal(key, -4.0, 4.0, (SUFFIX, D), jnp.float32) * (0.5 * 3.0 ** position)[None, :]
    return values.astype(jnp.bfloat16)


def block_levels(rng, extent, cuts, least, largest):
    def one(axis_at, shards_of):
        draws = jax.random.uniform(jax.random.fold_in(jax.random.fold_in(rng, 6), axis_at), (shards_of,), jnp.float32, least / len(cuts), largest / len(cuts))
        return jnp.repeat(jnp.exp(draws), extent[axis_at] // shards_of).reshape((-1,) + (1,) * (len(extent) - axis_at - 1))

    factor_of = one(*cuts[0])
    for cut in cuts[1:]:
        factor_of = factor_of * one(*cut)
    return factor_of


def centred(own_key, dims, width, most, pieces=(), held_as=jnp.bfloat16):
    gain = block_levels(own_key, dims, pieces, -0.22, 0.18) if pieces else 1.0
    result = jax.random.normal(own_key, dims, jnp.float32) * width * gain
    return jnp.minimum(jnp.maximum(result, -most), most).astype(held_as)


def setup_inputs(seed: int = 0) -> dict:
    streams_of = jax.random.split(jax.random.key(seed), 11)
    queries = draw_queries(jax.random.fold_in(streams_of[10], 71), 0)
    suffix_kv = centred(streams_of[1], (SUFFIX, KVH * 2 * HD), 1.0, 6.0, ((0, 32), (1, 8)))
    cache = draw_cache(jax.random.fold_in(streams_of[10], 71), 0)
    block_list = draw_block_list(jax.random.fold_in(streams_of[10], 71), 0)
    counts = draw_counts(jax.random.fold_in(streams_of[10], 71), 0)
    out_weight = centred(streams_of[5], (HQ * HD, D), 0.4, 2.390625, ((0, 8), (1, 32)))
    residual = draw_residual(jax.random.fold_in(streams_of[10], 71), 0)
    norm_gain = jnp.clip(1.0 + 0.18 * jax.random.normal(streams_of[7], (D,), jnp.float32), 0.099609375, 1.8984375).astype(jnp.bfloat16)
    gate_weight = centred(streams_of[8], (D, FF), D ** -0.5, 0.0625, ((1, 32),))
    up_weight = centred(streams_of[9], (D, FF), D ** -0.5, 0.0625, ((1, 32),))
    return {"queries": queries, "suffix_kv": suffix_kv, "cache": cache, "block_list": block_list, "counts": counts, "out_weight": out_weight, "residual": residual, "norm_gain": norm_gain, "gate_weight": gate_weight, "up_weight": up_weight}


def reference(queries, suffix_kv, cache, block_list, counts, out_weight, residual, norm_gain, gate_weight, up_weight):
    score_scale = float(HD) ** (-0.5)
    group_ids = jnp.arange(N_STORE, dtype=jnp.int32)[:, None]
    chosen = cache[group_ids, block_list.astype(jnp.int32)]
    prefix_rows = N_STORE * CAP * BLK
    held_rows = jnp.arange(CAP, dtype=jnp.int32)[None, :] < counts.astype(jnp.int32)[:, None]
    held_rows = jnp.broadcast_to(held_rows[:, :, None], (N_STORE, CAP, BLK)).reshape(prefix_rows)
    prefix = chosen.reshape(prefix_rows, KVH, 2, HD)
    suffix = suffix_kv.reshape(SUFFIX, KVH, 2, HD)
    key_all = jnp.concatenate([prefix[:, :, 0], suffix[:, :, 0]], 0).transpose(1, 0, 2)
    value_all = jnp.concatenate([prefix[:, :, 1], suffix[:, :, 1]], 0).transpose(1, 0, 2)
    visible = jnp.concatenate([held_rows, jnp.ones((SUFFIX,), bool)])
    key_pos = jnp.concatenate([jnp.full((prefix_rows,), -1, jnp.int32), jnp.arange(SUFFIX, dtype=jnp.int32)])
    block_rows = min(512, SUFFIX)
    block_count = SUFFIX // block_rows
    query_all = queries.reshape(block_count, block_rows, KVH, GQ, HD).transpose(2, 0, 1, 3, 4)

    def per_head(member):
        query_head, key_head, value_head = member
        key_float = key_head.astype(jnp.float32)
        value_float = value_head.astype(jnp.float32)

        def per_block(block_member):
            query_block, block_index = block_member
            query_pos = block_index * block_rows + jnp.arange(block_rows, dtype=jnp.int32)
            scores = jnp.einsum('bgd,nd->bgn', query_block.astype(jnp.float32), key_float) * score_scale
            allowed = (visible[None, :] & (key_pos[None, :] <= query_pos[:, None]))[:, None, :]
            scores = jnp.where(allowed, scores, -1e+30)
            highest = lax.optimization_barrier(jnp.max(scores, axis=-1, keepdims=True))
            probs = jnp.where(allowed, jnp.exp(scores - highest), 0.0)
            total = lax.optimization_barrier(jnp.sum(probs, axis=-1))
            weights = lax.optimization_barrier(probs.astype(jnp.bfloat16)).astype(jnp.float32)
            summed = jnp.einsum('bgn,nd->bgd', weights, value_float)
            return (summed / total[..., None]).astype(jnp.bfloat16)
        return lax.map(per_block, (query_head, jnp.arange(block_count, dtype=jnp.int32)))
    attended = lax.map(per_head, (query_all, key_all, value_all))
    attended = attended.transpose(1, 2, 0, 3, 4).reshape(SUFFIX, HQ * HD)
    group_inputs = HQ * HD // N_STORE

    def add_group(running, group_index):
        begin = (group_index * group_inputs).astype(jnp.int32)
        columns = lax.dynamic_slice_in_dim(attended, begin, group_inputs, 1)
        weight_rows = lax.dynamic_slice_in_dim(out_weight, begin, group_inputs, 0)
        partial_value = jnp.dot(columns, weight_rows, preferred_element_type=jnp.float32)
        partial_value = lax.optimization_barrier(partial_value.astype(jnp.bfloat16)).astype(jnp.float32)
        return (running + partial_value, None)
    projected, unused = lax.scan(add_group, jnp.zeros((SUFFIX, D), jnp.float32), jnp.arange(N_STORE, dtype=jnp.int32))
    hidden_state = (residual.astype(jnp.float32) + projected).astype(jnp.bfloat16)
    h_float = hidden_state.astype(jnp.float32)
    squares = lax.optimization_barrier(jnp.sum(h_float * h_float, axis=-1, keepdims=True))
    normed = (h_float * lax.rsqrt(squares / D + 1e-05) * norm_gain.astype(jnp.float32)[None, :]).astype(jnp.bfloat16)
    gate_sum = jnp.dot(normed, gate_weight, preferred_element_type=jnp.float32)
    up_sum = jnp.dot(normed, up_weight, preferred_element_type=jnp.float32)
    swiglu = (jax.nn.silu(gate_sum) * up_sum).astype(jnp.bfloat16)
    return (hidden_state, swiglu)
```

```python
import functools
import math

import jax
import jax.numpy as jnp
from jax import lax
from jax.experimental import pallas as pl
from jax.experimental.pallas import tpu as pltpu
from jax.sharding import PartitionSpec as P

D = 7168
HD = 128
GQ = 7
SCALE2 = float(HD) ** (-0.5) * math.log2(math.e)
NT = (((1,), (1,)), ((), ()))
NN = (((1,), (0,)), ((), ()))

OFF = (0, -1, 1, 2)


def cidx(h, y, x):
    return (h % 2) * 16 + (y % 4) * 4 + (x % 4)


PLACES = [(h, y, x) for h in range(2) for y in range(4) for x in range(4)]


def shift_x(v, k):
    return lax.ppermute(v, "ctx", [(cidx(h, y, x), cidx(h, y, x + k)) for h, y, x in PLACES])


def shift_y(v, k):
    return lax.ppermute(v, "ctx", [(cidx(h, y, x), cidx(h, y + k, x)) for h, y, x in PLACES])


def swap_h(v):
    return lax.ppermute(v, "ctx", [(cidx(h, y, x), cidx(h + 1, y, x)) for h, y, x in PLACES])


def shift_z(v, k):
    pairs = []
    for s in range(8):
        for h, y, x in PLACES:
            z = (h * 4 + s // 2 + k) % 8
            pairs.append((s * 32 + cidx(h, y, x), (z % 4 * 2 + s % 2) * 32 + cidx(z // 4, y, x)))
    return lax.ppermute(v, ("store", "ctx"), pairs)


def swap_core(v):
    return lax.ppermute(v, "store", [(s, s ^ 1) for s in range(8)])


def z_gather(v):
    half = v.shape[0] // 2
    up1, dn1 = shift_z(v, 1), shift_z(v, -1)
    up2, dn2 = shift_z(up1, 1), shift_z(dn1, -1)
    up3, dn3 = shift_z(up2, 1), shift_z(dn2, -1)
    up4, dn4 = shift_z(up3[:half], 1), shift_z(dn3[half:], -1)
    return v, up1, dn1, up2, dn2, up3, dn3, up4, dn4


def gather(v, first, second):
    row = jnp.concatenate([v, first(v, 1), first(v, -1), first(v, 2)])
    up, dn = second(row, 1), second(row, -1)
    return row, up, dn, second(up[:2], 1), second(dn[2:], -1)


def plane_gather(a, b):
    return gather(a[None], shift_x, shift_y), gather(b[None], shift_y, shift_x)


def pieces_of(refs):
    for outer in range(3):
        for inner in range(4):
            yield refs[outer], inner, OFF[outer], OFF[inner]
    for inner in range(4):
        yield refs[3 + inner // 2], inner % 2, 2, OFF[inner]


def spots_of(where, refs, swapped):
    y, x = where[1], where[2]
    for ref, at, outer, inner in pieces_of(refs):
        dy, dx = (inner, outer) if swapped else (outer, inner)
        yield ref, at, ((y + dy) & 3) * 4 + ((x + dx) & 3)


def load_keys(where, a_refs, b_refs, keys, values):
    for group, swapped, out in ((a_refs, False, keys), (b_refs, True, values)):
        for ref, at, spot in spots_of(where, group, swapped):
            for j in range(4):
                place = ((where[0] + j) & 1) * 16 + spot + j // 2 * 32
                out[pl.ds(pl.multiple_of(place * 128, 128), 128), :] = ref[at, j]


def absorb(scores, value, top, total, acc):
    new_top = jnp.maximum(top, jnp.max(scores, axis=1, keepdims=True))
    factor = jnp.exp2(top - new_top)
    probs = jnp.exp2(scores - new_top)
    total = total * factor + jnp.sum(probs, axis=1, keepdims=True)
    acc = acc * factor + lax.dot_general(
        probs.astype(jnp.bfloat16), value, NN, preferred_element_type=jnp.float32
    )
    return new_top, total, acc


def attend_kernel(where, q_ref, *refs):
    a_refs, b_refs = refs[:5], refs[5:10]
    out_ref, keys, values, acc_ref, top_ref, total_ref = refs[10:]
    load_keys(where, a_refs, b_refs, keys, values)
    me = where[0] * 16 + where[1] * 4 + where[2]
    acc_ref[...] = jnp.zeros_like(acc_ref)
    top_ref[...] = jnp.full_like(top_ref, -1e30)
    total_ref[...] = jnp.zeros_like(total_ref)
    span = 16 * GQ
    row = lax.broadcasted_iota(jnp.int32, (span, 512), 0)
    col = lax.broadcasted_iota(jnp.int32, (span, 512), 1)
    token = (row * 9363) >> 16
    allowed = col <= (token >> 2) * 128 + (token & 3) + 4 * me
    for m in range(8):
        r0 = span * m
        key = keys[512 * m : 512 * (m + 1), :]
        value = values[512 * m : 512 * (m + 1), :]
        parts = [(r0, r0 + span, True)]
        if m < 7:
            parts.append((r0 + span, 8 * span, False))
        for lo, hi, masked in parts:
            scores = (
                lax.dot_general(q_ref[lo:hi, :], key, NT, preferred_element_type=jnp.float32)
                * SCALE2
            )
            if masked:
                scores = jnp.where(allowed, scores, -1e30)
            top, total, acc = absorb(
                scores, value, top_ref[lo:hi, :], total_ref[lo:hi, :], acc_ref[lo:hi, :]
            )
            top_ref[lo:hi, :] = top
            total_ref[lo:hi, :] = total
            acc_ref[lo:hi, :] = acc
    rows = 448
    for lo in range(0, 896, rows):
        hi = lo + rows
        top, total, acc = top_ref[lo:hi, :], total_ref[lo:hi, :], acc_ref[lo:hi, :]
        for n in range(4, 8):
            key = keys[1024 * n : 1024 * (n + 1), :]
            value = values[1024 * n : 1024 * (n + 1), :]
            scores = (
                lax.dot_general(q_ref[lo:hi, :], key, NT, preferred_element_type=jnp.float32)
                * SCALE2
            )
            top, total, acc = absorb(scores, value, top, total, acc)
        out_ref[lo:hi, :] = (acc / total).astype(jnp.bfloat16)


def out_kernel(where, resid_ref, *refs):
    w_refs, a_refs, b_refs = refs[:12], refs[12:17], refs[17:22]
    hid_ref, xs, acc_ref = refs[22:]
    for base, group, swapped in ((0, a_refs, False), (4, b_refs, True)):
        for ref, at, spot in spots_of(where, group, swapped):
            xs[base : base + 4, pl.ds(pl.multiple_of(spot * 16, 16), 16), :] = ref[at]
    acc_ref[...] = jnp.zeros_like(acc_ref)

    def add(weight, offset, other_core, rows):
        z = (where[4] + offset) & 7
        core = where[5] ^ other_core
        acc_ref[z >> 2, rows, :] += lax.dot_general(
            weight, xs[(z & 3) * 2 + core], NT, preferred_element_type=jnp.float32
        )

    low_rows, high_rows, all_rows = slice(0, 112), slice(112, 224), slice(0, 224)
    for i, offset in enumerate((0, -1, 1, -2, 2, -3, 3)):
        add(w_refs[i][...], offset, 0, all_rows)
        add(w_refs[9][i], offset, 1, all_rows)
    for own, far, rows in ((7, 10, low_rows), (8, 11, high_rows)):
        add(w_refs[own][...], 4, 0, rows)
        add(w_refs[far][...], 4, 1, rows)
    for h in range(2):
        hid_ref[h] = (acc_ref[h] + resid_ref[h].astype(jnp.float32)).astype(jnp.bfloat16)


def ffn_kernel(swapped, where, gate_ref, up_ref, gain_ref, *refs):
    out_ref, xs = refs[5:]
    squares = jnp.zeros((8, 256), jnp.float32)
    for ref, at, spot in spots_of(where, refs[:5], swapped):
        for h in range(2):
            piece = ref[at, h]
            xs[pl.ds(pl.multiple_of(h * 3584 + spot * 224, 32), 224), :] = piece
            wide = piece.astype(jnp.float32)
            squares += jnp.sum((wide * wide).reshape(28, 8, 256), axis=0)
    inverse = lax.rsqrt(jnp.sum(squares, axis=0, keepdims=True) / D + 1e-05)
    for i in range(16):
        rows = slice(448 * i, 448 * (i + 1))
        xs[rows, :] = (
            xs[rows, :].astype(jnp.float32) * inverse * gain_ref[rows, :].astype(jnp.float32)
        ).astype(jnp.bfloat16)
    gate = lax.dot_general(gate_ref[...], xs[...], NN, preferred_element_type=jnp.float32)
    up = lax.dot_general(up_ref[...], xs[...], NN, preferred_element_type=jnp.float32)
    out_ref[...] = (gate / (1.0 + jnp.exp(-gate)) * up).astype(jnp.bfloat16)


SMEM = pl.BlockSpec(memory_space=pltpu.SMEM)
VMEM = pl.BlockSpec(memory_space=pltpu.VMEM)


def call(body, out_shape, scratch, n_vmem, flops):
    many = isinstance(out_shape, (tuple, list))
    return pl.pallas_call(
        body,
        out_shape=out_shape,
        in_specs=[SMEM] + [VMEM] * n_vmem,
        out_specs=[VMEM] * len(out_shape) if many else VMEM,
        scratch_shapes=scratch,
        compiler_params=pltpu.CompilerParams(vmem_limit_bytes=40 * 1024 * 1024),
        cost_estimate=pl.CostEstimate(flops=flops, bytes_accessed=0, transcendentals=0),
    )


def local(
    queries,
    suffix_kv,
    cache,
    block_list,
    counts,
    out_weight,
    residual,
    norm_gain,
    gate_weight,
    up_weight,
):
    bf16, f32 = jnp.bfloat16, jnp.float32
    place = lax.axis_index("ctx")
    zh, y, x = place // 16, place // 4 % 4, place % 4
    store = lax.axis_index("store")
    where = jnp.stack([zh, y, x, place, zh * 4 + store // 2, store % 2]).astype(jnp.int32)

    with jax.named_scope("prefix"):
        chosen = jnp.take(cache[0], block_list[0], axis=0, mode="clip")
        chosen = chosen.reshape(32, 8, 2 * HD).transpose(1, 0, 2)
        groups = [
            [s * 32 + cidx(h, yy, xx) for h in range(2) for s in range(8)]
            for yy in range(4)
            for xx in range(4)
        ]
        fetched = lax.all_to_all(
            jnp.concatenate([chosen, chosen]),
            ("store", "ctx"),
            split_axis=0,
            concat_axis=0,
            tiled=True,
            axis_index_groups=groups,
        )
        eight = jnp.arange(8, dtype=jnp.int32)
        slot = jnp.arange(32, dtype=jnp.int32)
        ends = jnp.sum(jnp.where(eight[None, :] <= eight[:, None], counts[None, :], 0), axis=1)
        group = jnp.sum((slot[:, None] >= ends[None, :]).astype(jnp.int32), axis=1)
        begin = jnp.sum(jnp.where(eight[None, :] < group[:, None], counts[None, :], 0), axis=1)
        pick = group * 8 + slot - begin
        pick = jnp.concatenate([pick, pick + 64])
        real = jnp.take(fetched.reshape(128, 4, 2 * HD), pick, axis=0, mode="clip")
        real = real.reshape(2, 128, 2 * HD)

    with jax.named_scope("keys"):
        both = jnp.concatenate([suffix_kv[None], swap_h(suffix_kv)[None], real])
        kv_a, kv_b = plane_gather(both[:, :, :HD], both[:, :, HD:])

    with jax.named_scope("queries"):
        gain_part = jnp.broadcast_to(jnp.pad(norm_gain, (0, 288)).reshape(1, 4, HD), (32, 4, HD))
        zero = jnp.minimum(jnp.abs(kv_a[1][0, 0, 0, 0]), 0)
        sent = jnp.concatenate([queries.reshape(32, 4, GQ * HD), gain_part], axis=2) + zero
        came = lax.all_to_all(sent, "ctx", split_axis=0, concat_axis=0, tiled=True)
        q = came[:, :, : GQ * HD].reshape(128 * GQ, HD)
        gain_all = came[:, :, GQ * HD :].reshape(32, 4 * HD)[:, :224].reshape(D, 1)

    with jax.named_scope("weights"):
        w_own = z_gather(out_weight.T)
        w_near = swap_core(jnp.stack(w_own[:7]))
        w_all = (*w_own, w_near, swap_core(w_own[7]), swap_core(w_own[8]))

    with jax.named_scope("order"):
        half = jnp.arange(256, dtype=jnp.int32)
        half = half // 4 % 4 * 128 + half // 16 * 4 + half % 4
        half = jnp.concatenate([half + 64 * zh, half + 64 * (1 - zh)])
        order = (half[:, None] == jnp.arange(512, dtype=jnp.int32)[None, :]).astype(bf16)
        resid = lax.dot_general(
            residual.T, order, NT, preferred_element_type=f32
        ).astype(bf16)
        mine, theirs = resid[:, :256], swap_h(resid[:, 256:])
        resid = jnp.where(zh == 0, jnp.stack([mine, theirs]), jnp.stack([theirs, mine]))

    with jax.named_scope("attend"):
        attended = call(
            attend_kernel,
            jax.ShapeDtypeStruct((896, HD), bf16),
            [
                pltpu.VMEM((8192, HD), bf16),
                pltpu.VMEM((8192, HD), bf16),
                pltpu.VMEM((896, HD), f32),
                pltpu.VMEM((896, 1), f32),
                pltpu.VMEM((896, 1), f32),
            ],
            11,
            flops=20 * 10**9,
        )(where, q, *kv_a, *kv_b)

    with jax.named_scope("project"):
        sent = lax.all_to_all(
            attended.reshape(8, 16, GQ * HD), "store", split_axis=0, concat_axis=0, tiled=True
        )
        att_a, att_b = plane_gather(sent[:4], sent[4:])
        hid = call(
            out_kernel,
            jax.ShapeDtypeStruct((2, 224, 256), bf16),
            [pltpu.VMEM((8, 256, GQ * HD), bf16), pltpu.VMEM((2, 224, 256), f32)],
            23,
            flops=6 * 10**9,
        )(where, resid, *w_all, *att_a, *att_b)

    with jax.named_scope("feed"):
        def ffn(pieces, swapped):
            return call(
                functools.partial(ffn_kernel, swapped),
                jax.ShapeDtypeStruct((320, 256), bf16),
                [pltpu.VMEM((D, 256), bf16)],
                8,
                flops=7 * 10**9,
            )(where, gate_weight.T, up_weight.T, gain_all, *pieces)

        other = swap_h(hid)
        near = ffn(gather(hid[None], shift_x, shift_y), False)
        far = ffn(gather(other[None], shift_y, shift_x), True)
        pair = jnp.concatenate(
            [jnp.where(zh == 0, hid[0], hid[1]), jnp.where(zh == 0, other[0], other[1])], axis=1
        )
        hidden_state = jnp.dot(pair, order, preferred_element_type=f32).astype(bf16).T
        both = jnp.concatenate([near, far], axis=1)
        swiglu = jnp.dot(both, order, preferred_element_type=f32).astype(bf16).T
    return (hidden_state, swiglu)


def solution(mesh):
    return jax.shard_map(
        local,
        mesh=mesh,
        in_specs=(
            P("ctx", "store"),
            P("ctx", "store"),
            P("store", None, "ctx", None),
            P("store", None),
            P(),
            P("store", "ctx"),
            P("store", "ctx"),
            P("ctx"),
            P(None, "ctx"),
            P(None, "ctx"),
        ),
        out_specs=(P("store", "ctx"), P("store", "ctx")),
        check_vma=False,
    )
```

```python
import functools
import math

import jax
import jax.numpy as jnp
from jax import lax
from jax.experimental import pallas as pl
from jax.experimental.pallas import tpu as pltpu
from jax.sharding import PartitionSpec as P

D = 7168
HD = 128
GQ = 7
SCALE2 = float(HD) ** (-0.5) * math.log2(math.e)
NT = (((1,), (1,)), ((), ()))
NN = (((1,), (0,)), ((), ()))
TN = (((0,), (0,)), ((), ()))

OFF = (0, -1, 1, 2)


def cidx(h, y, x):
    return (h % 2) * 16 + (y % 4) * 4 + (x % 4)


PLACES = [(h, y, x) for h in range(2) for y in range(4) for x in range(4)]


def shift_x(v, k):
    return lax.ppermute(v, "ctx", [(cidx(h, y, x), cidx(h, y, x + k)) for h, y, x in PLACES])


def shift_y(v, k):
    return lax.ppermute(v, "ctx", [(cidx(h, y, x), cidx(h, y + k, x)) for h, y, x in PLACES])


def swap_h(v):
    return lax.ppermute(v, "ctx", [(cidx(h, y, x), cidx(h + 1, y, x)) for h, y, x in PLACES])


def shift_z(v, k):
    pairs = []
    for s in range(8):
        for h, y, x in PLACES:
            z = (h * 4 + s // 2 + k) % 8
            pairs.append((s * 32 + cidx(h, y, x), (z % 4 * 2 + s % 2) * 32 + cidx(z // 4, y, x)))
    return lax.ppermute(v, ("store", "ctx"), pairs)


def swap_core(v):
    return lax.ppermute(v, "store", [(s, s ^ 1) for s in range(8)])


def z_gather(v):
    half = v.shape[0] // 2
    up1, dn1 = shift_z(v, 1), shift_z(v, -1)
    up2, dn2 = shift_z(up1, 1), shift_z(dn1, -1)
    up3, dn3 = shift_z(up2, 1), shift_z(dn2, -1)
    up4, dn4 = shift_z(up3[:half], 1), shift_z(dn3[half:], -1)
    return v, up1, dn1, up2, dn2, up3, dn3, up4, dn4


def nothing(v):
    return jnp.where(jnp.abs(v) > 1e30, v, 0)


def gather(v, first, second):
    low = jnp.concatenate([v, first(v, 1)])
    high = jnp.concatenate([first(v, -1), first(v, 2)])
    up_low, up_high = second(low, 1), second(high, 1)
    dn_low, dn_high = second(low, -1), second(high, -1)
    return low, high, up_low, up_high, dn_low, dn_high, second(up_low, 1), second(dn_high, -1)


def plane_gather(a, b):
    return gather(a[None], shift_x, shift_y), gather(b[None], shift_y, shift_x)


def pieces_of(refs):
    for i, ref in enumerate(refs):
        for at in range(2):
            yield ref, at, OFF[i // 2], OFF[i % 2 * 2 + at]


def spots_of(where, refs, swapped):
    y, x = where[1], where[2]
    for ref, at, outer, inner in pieces_of(refs):
        dy, dx = (inner, outer) if swapped else (outer, inner)
        yield ref, at, ((y + dy) & 3) * 4 + ((x + dx) & 3)


def fetch(where, refs, swapped, place_of, sems, first_sem):
    copies = []
    for i, (ref, at, spot) in enumerate(spots_of(where, refs, swapped)):
        copy = pltpu.make_async_copy(ref.at[at], place_of(spot), sems.at[first_sem + i])
        copy.start()
        copies.append(copy)
    return copies


STEPS = [(n % 4, n // 4, 0, None) for n in range(8)]
STEPS += [(m % 4, m // 4, 112 * m // 128 * 128, m) for m in range(8)]


def attend_kernel(where, q_ref, *refs):
    a_refs, b_refs = refs[:8], refs[8:16]
    out_ref, keys, values, acc_ref, top_ref, total_ref, sems = refs[16:]
    copies = fetch(where, a_refs, False, lambda spot: keys.at[spot], sems, 0)
    copies += fetch(where, b_refs, True, lambda spot: values.at[spot], sems, 16)
    for copy in copies:
        copy.wait()
    me = where[3]
    key_row = lax.broadcasted_iota(jnp.int32, (512, 256), 0)
    query_row = lax.broadcasted_iota(jnp.int32, (512, 256), 1)

    def rows_of(buffer, step):
        row, end, _, m = step
        part = end + 2 if m is None else (where[0] ^ end)
        return buffer[4 * row : 4 * row + 4, part].reshape(512, HD)

    def scores_of(step):
        return lax.dot_general(
            rows_of(keys, step), q_ref[step[2] :, :], NT, preferred_element_type=jnp.float32
        )

    ready = [scores_of(STEPS[0]), scores_of(STEPS[1])]
    for i, step in enumerate(STEPS):
        lo, m = step[2:]
        scores = ready.pop(0)
        if i + 2 < len(STEPS):
            ready.append(scores_of(STEPS[i + 2]))
        if m is not None:
            wide = min(256, 896 - lo)
            token = ((query_row[:, :wide] + (lo - 112 * m + 112)) * 9363 >> 16) - 16
            allowed = key_row[:, :wide] <= (token >> 2) * 128 + (token & 3) + 4 * me
            masked = jnp.where(allowed, scores[:, :wide], -1e30)
            scores = (
                jnp.concatenate([masked, scores[:, wide:]], axis=1) if lo + wide < 896 else masked
            )
        top = jnp.max(scores, axis=0, keepdims=True) * SCALE2
        if i > 0:
            old = top_ref[:, lo:]
            top = jnp.maximum(old, top)
            factor = jnp.exp2(old - top)
        probs = jnp.exp2(scores * SCALE2 - top)
        total = jnp.sum(probs, axis=0, keepdims=True)
        acc = lax.dot_general(
            rows_of(values, step),
            probs.astype(jnp.bfloat16),
            TN,
            preferred_element_type=jnp.float32,
        )
        if i > 0:
            total += total_ref[:, lo:] * factor
            acc += acc_ref[:, lo:] * factor
        top_ref[:, lo:] = top
        total_ref[:, lo:] = total
        acc_ref[:, lo:] = acc
    out_ref[...] = (acc_ref[...] / total_ref[...]).T.astype(jnp.bfloat16)


def out_kernel(where, resid_ref, *refs):
    w_refs, a_refs, b_refs = refs[:12], refs[12:20], refs[20:28]
    hid_ref, xs, w_own, w_other, acc_ref, sems = refs[28:]
    low_rows, high_rows = pl.ds(0, 112), pl.ds(112, 112)
    targets = [w_own.at[i] for i in range(7)]
    targets += [w_own.at[7, low_rows], w_own.at[7, high_rows], w_other.at[pl.ds(0, 7)]]
    targets += [w_other.at[7, low_rows], w_other.at[7, high_rows]]
    copies = fetch(where, a_refs, False, lambda spot: xs.at[pl.ds(0, 4), spot], sems, 0)
    copies += fetch(where, b_refs, True, lambda spot: xs.at[pl.ds(4, 4), spot], sems, 16)
    for i in range(12):
        copy = pltpu.make_async_copy(w_refs[i], targets[i], sems.at[32 + i])
        copy.start()
        copies.append(copy)
    for h in range(2):
        acc_ref[h] = resid_ref[h].astype(jnp.float32)
    for copy in copies:
        copy.wait()
    for i, offset in enumerate((0, -1, 1, -2, 2, -3, 3, 4)):
        z = (where[4] + offset) & 7
        for other, buffer in enumerate((w_own, w_other)):
            x = xs[(z & 3) * 2 + (where[5] ^ other)].reshape(256, GQ * HD)
            acc_ref[z >> 2] += lax.dot_general(
                buffer[i], x, NT, preferred_element_type=jnp.float32
            )
    for h in range(2):
        hid_ref[h] = acc_ref[h].astype(jnp.bfloat16)


def ffn_kernel(swapped, where, gate_ref, up_ref, gain_ref, *refs):
    out_ref, xs = refs[8:]
    squares = jnp.zeros((8, 256), jnp.float32)
    for ref, at, spot in spots_of(where, refs[:8], swapped):
        for h in range(2):
            rows = pl.ds(pl.multiple_of(h * 3584 + spot * 224, 32), 224)
            wide = ref[at, h].astype(jnp.float32)
            xs[rows, :] = (wide * gain_ref[rows, :].astype(jnp.float32)).astype(jnp.bfloat16)
            squares += jnp.sum((wide * wide).reshape(28, 8, 256), axis=0)
    inverse = lax.rsqrt(jnp.sum(squares, axis=0, keepdims=True) / D + 1e-05)
    gate = lax.dot_general(gate_ref[...], xs[...], NN, preferred_element_type=jnp.float32)
    gate *= inverse
    up = lax.dot_general(up_ref[...], xs[...], NN, preferred_element_type=jnp.float32)
    out_ref[...] = (gate / (1.0 + jnp.exp(-gate)) * (up * inverse)).astype(jnp.bfloat16)


SMEM = pl.BlockSpec(memory_space=pltpu.SMEM)
VMEM = pl.BlockSpec(memory_space=pltpu.VMEM)
ANY = pl.BlockSpec(memory_space=pl.ANY)


def call(body, out_shape, scratch, specs, flops, mib=12):
    many = isinstance(out_shape, (tuple, list))
    return pl.pallas_call(
        body,
        out_shape=out_shape,
        in_specs=[SMEM] + specs,
        out_specs=[VMEM] * len(out_shape) if many else VMEM,
        scratch_shapes=scratch,
        compiler_params=pltpu.CompilerParams(vmem_limit_bytes=mib * 1024 * 1024),
        cost_estimate=pl.CostEstimate(flops=flops, bytes_accessed=0, transcendentals=0),
    )


def local(
    queries,
    suffix_kv,
    cache,
    block_list,
    counts,
    out_weight,
    residual,
    norm_gain,
    gate_weight,
    up_weight,
):
    bf16, f32 = jnp.bfloat16, jnp.float32
    place = lax.axis_index("ctx")
    zh, y, x = place // 16, place // 4 % 4, place % 4
    store = lax.axis_index("store")
    where = jnp.stack([zh, y, x, place, zh * 4 + store // 2, store % 2]).astype(jnp.int32)

    with jax.named_scope("prefix"):
        chosen = jnp.take(cache[0], block_list[0], axis=0, mode="clip")
        chosen = chosen.reshape(32, 8, 2 * HD).transpose(1, 0, 2)
        groups = [
            [s * 32 + cidx(h, yy, xx) for h in range(2) for s in range(8)]
            for yy in range(4)
            for xx in range(4)
        ]
        fetched = lax.all_to_all(
            jnp.concatenate([chosen, chosen]),
            ("store", "ctx"),
            split_axis=0,
            concat_axis=0,
            tiled=True,
            axis_index_groups=groups,
        )
        eight = jnp.arange(8, dtype=jnp.int32)
        slot = jnp.arange(32, dtype=jnp.int32)
        ends = jnp.sum(jnp.where(eight[None, :] <= eight[:, None], counts[None, :], 0), axis=1)
        group = jnp.sum((slot[:, None] >= ends[None, :]).astype(jnp.int32), axis=1)
        begin = jnp.sum(jnp.where(eight[None, :] < group[:, None], counts[None, :], 0), axis=1)
        pick = group * 8 + slot - begin
        pick = jnp.concatenate([pick, pick + 64])
        real = jnp.take(fetched.reshape(128, 4, 2 * HD), pick, axis=0, mode="clip")
        real = real.reshape(2, 128, 2 * HD)

    with jax.named_scope("keys"):
        both = jnp.concatenate([suffix_kv[None], swap_h(suffix_kv)[None], real])
        kv_a, kv_b = plane_gather(both[:, :, :HD], both[:, :, HD:])

    with jax.named_scope("queries"):
        gain_part = jnp.broadcast_to(jnp.pad(norm_gain, (0, 288)).reshape(1, 4, HD), (32, 4, HD))
        sent = jnp.concatenate([queries.reshape(32, 4, GQ * HD), gain_part], axis=2)
        sent += nothing(kv_a[2][0, 0, 0, 0])
        came = lax.all_to_all(sent, "ctx", split_axis=0, concat_axis=0, tiled=True)
        q = came[:, :, : GQ * HD].reshape(128 * GQ, HD)
        gain_all = came[:, :, GQ * HD :].reshape(32, 4 * HD)[:, :224].reshape(D, 1)

    with jax.named_scope("weights"):
        w_own = z_gather(out_weight.T)
        w_near = swap_core(jnp.stack(w_own[:7]))
        w_all = (*w_own, w_near, swap_core(w_own[7]), swap_core(w_own[8]))

    with jax.named_scope("order"):
        half = jnp.arange(256, dtype=jnp.int32)
        half = half // 4 % 4 * 128 + half // 16 * 4 + half % 4
        half = jnp.concatenate([half + 64 * zh, half + 64 * (1 - zh)])
        order = (half[:, None] == jnp.arange(512, dtype=jnp.int32)[None, :]).astype(bf16)
        resid = lax.dot_general(
            residual.T, order, NT, preferred_element_type=f32
        ).astype(bf16)
        mine, theirs = resid[:, :256], swap_h(resid[:, 256:])
        resid = jnp.where(zh == 0, jnp.stack([mine, theirs]), jnp.stack([theirs, mine]))

    with jax.named_scope("attend"):
        attended = call(
            attend_kernel,
            jax.ShapeDtypeStruct((896, HD), bf16),
            [
                pltpu.VMEM((16, 4, 128, HD), bf16),
                pltpu.VMEM((16, 4, 128, HD), bf16),
                pltpu.VMEM((HD, 896), f32),
                pltpu.VMEM((1, 896), f32),
                pltpu.VMEM((1, 896), f32),
                pltpu.SemaphoreType.DMA((32,)),
            ],
            [VMEM] + [ANY] * 16,
            flops=20 * 10**9,
            mib=24,
        )(where, q, *kv_a, *kv_b)

    with jax.named_scope("project"):
        sent = lax.all_to_all(
            attended.reshape(8, 16, GQ * HD), "store", split_axis=0, concat_axis=0, tiled=True
        )
        att_a, att_b = plane_gather(sent[:4], sent[4:])
        hid = call(
            out_kernel,
            jax.ShapeDtypeStruct((2, 224, 256), bf16),
            [
                pltpu.VMEM((8, 16, 16, GQ * HD), bf16),
                pltpu.VMEM((8, 224, GQ * HD), bf16),
                pltpu.VMEM((8, 224, GQ * HD), bf16),
                pltpu.VMEM((2, 224, 256), f32),
                pltpu.SemaphoreType.DMA((44,)),
            ],
            [VMEM] + [ANY] * 28,
            flops=6 * 10**9,
            mib=20,
        )(where, resid, *w_all, *att_a, *att_b)

    with jax.named_scope("feed"):
        def ffn(pieces, swapped):
            return call(
                functools.partial(ffn_kernel, swapped),
                jax.ShapeDtypeStruct((320, 256), bf16),
                [pltpu.VMEM((D, 256), bf16)],
                [VMEM] * 11,
                flops=7 * 10**9,
            )(where, gate_weight.T, up_weight.T, gain_all, *pieces)

        other = swap_h(hid)
        near = ffn(gather(hid[None], shift_x, shift_y), False)
        far = ffn(gather(other[None], shift_y, shift_x), True)
        pair = jnp.concatenate(
            [jnp.where(zh == 0, hid[0], hid[1]), jnp.where(zh == 0, other[0], other[1])], axis=1
        )
        hidden_state = jnp.dot(pair, order, preferred_element_type=f32).astype(bf16).T
        both = jnp.concatenate([near, far], axis=1)
        swiglu = jnp.dot(both, order, preferred_element_type=f32).astype(bf16).T
    return (hidden_state, swiglu)


def solution(mesh):
    return jax.shard_map(
        local,
        mesh=mesh,
        in_specs=(
            P("ctx", "store"),
            P("ctx", "store"),
            P("store", None, "ctx", None),
            P("store", None),
            P(),
            P("store", "ctx"),
            P("store", "ctx"),
            P("ctx"),
            P(None, "ctx"),
            P(None, "ctx"),
        ),
        out_specs=(P("store", "ctx"), P("store", "ctx")),
        check_vma=False,
    )
```

```python
import functools
import math

import jax
import jax.numpy as jnp
from jax import lax
from jax.experimental import pallas as pl
from jax.experimental.pallas import tpu as pltpu
from jax.sharding import PartitionSpec as P

D = 7168
HD = 128
GQ = 7
SCALE2 = float(HD) ** (-0.5) * math.log2(math.e)
NT = (((1,), (1,)), ((), ()))
NN = (((1,), (0,)), ((), ()))
TN = (((0,), (0,)), ((), ()))

OFF = (0, -1, 1, 2)


def cidx(h, y, x):
    return (h % 2) * 16 + (y % 4) * 4 + (x % 4)


PLACES = [(h, y, x) for h in range(2) for y in range(4) for x in range(4)]


def shift_x(v, k):
    return lax.ppermute(v, "ctx", [(cidx(h, y, x), cidx(h, y, x + k)) for h, y, x in PLACES])


def shift_y(v, k):
    return lax.ppermute(v, "ctx", [(cidx(h, y, x), cidx(h, y + k, x)) for h, y, x in PLACES])


def swap_h(v):
    return lax.ppermute(v, "ctx", [(cidx(h, y, x), cidx(h + 1, y, x)) for h, y, x in PLACES])


def shift_z(v, k):
    pairs = []
    for s in range(8):
        for h, y, x in PLACES:
            z = (h * 4 + s // 2 + k) % 8
            pairs.append((s * 32 + cidx(h, y, x), (z % 4 * 2 + s % 2) * 32 + cidx(z // 4, y, x)))
    return lax.ppermute(v, ("store", "ctx"), pairs)


def swap_core(v):
    return lax.ppermute(v, "store", [(s, s ^ 1) for s in range(8)])


def z_gather(v):
    half = v.shape[0] // 2
    up1, dn1 = shift_z(v, 1), shift_z(v, -1)
    up2, dn2 = shift_z(up1, 1), shift_z(dn1, -1)
    up3, dn3 = shift_z(up2, 1), shift_z(dn2, -1)
    up4, dn4 = shift_z(up3[:half], 1), shift_z(dn3[half:], -1)
    return v, up1, dn1, up2, dn2, up3, dn3, up4, dn4


def nothing(v):
    return jnp.where(jnp.abs(v) > 1e30, v, 0)


def gather(v, first, second):
    low = jnp.concatenate([v, first(v, 1)])
    high = jnp.concatenate([first(v, -1), first(v, 2)])
    up_low, up_high = second(low, 1), second(high, 1)
    dn_low, dn_high = second(low, -1), second(high, -1)
    return low, high, up_low, up_high, dn_low, dn_high, second(up_low, 1), second(dn_high, -1)


def plane_gather(a, b):
    return gather(a[None], shift_x, shift_y), gather(b[None], shift_y, shift_x)


def pieces_of(refs):
    for i, ref in enumerate(refs):
        for at in range(2):
            yield ref, at, OFF[i // 2], OFF[i % 2 * 2 + at]


def spots_of(where, refs, swapped):
    y, x = where[1], where[2]
    for ref, at, outer, inner in pieces_of(refs):
        dy, dx = (inner, outer) if swapped else (outer, inner)
        yield ref, at, ((y + dy) & 3) * 4 + ((x + dx) & 3)


def fetch(where, refs, swapped, place_of, sems, first_sem):
    copies = []
    for i, (ref, at, spot) in enumerate(spots_of(where, refs, swapped)):
        copy = pltpu.make_async_copy(ref.at[at], place_of(spot), sems.at[first_sem + i])
        copy.start()
        copies.append(copy)
    return copies


STEPS = [(n % 4, n // 4, 0, None) for n in range(8)]
STEPS += [(m % 4, m // 4, 112 * m // 128 * 128, m) for m in range(8)]


def attend_kernel(where, q_ref, *refs):
    a_refs, b_refs = refs[:8], refs[8:16]
    out_ref, keys, values, acc_ref, top_ref, total_ref, sems = refs[16:]
    copies = fetch(where, a_refs, False, lambda spot: keys.at[spot], sems, 0)
    copies += fetch(where, b_refs, True, lambda spot: values.at[spot], sems, 16)
    for copy in copies:
        copy.wait()
    me = where[3]
    key_row = lax.broadcasted_iota(jnp.int32, (512, 256), 0)
    query_row = lax.broadcasted_iota(jnp.int32, (512, 256), 1)

    def rows_of(buffer, step):
        row, end, _, m = step
        part = end + 2 if m is None else (where[0] ^ end)
        return buffer[4 * row : 4 * row + 4, part].reshape(512, HD)

    def scores_of(step):
        return lax.dot_general(
            rows_of(keys, step), q_ref[step[2] :, :], NT, preferred_element_type=jnp.float32
        )

    ready = [scores_of(STEPS[0]), scores_of(STEPS[1])]
    for i, step in enumerate(STEPS):
        lo, m = step[2:]
        scores = ready.pop(0)
        if i + 2 < len(STEPS):
            ready.append(scores_of(STEPS[i + 2]))
        if m is not None:
            wide = min(256, 896 - lo)
            token = ((query_row[:, :wide] + (lo - 112 * m + 112)) * 9363 >> 16) - 16
            allowed = key_row[:, :wide] <= (token >> 2) * 128 + (token & 3) + 4 * me
            masked = jnp.where(allowed, scores[:, :wide], -1e30)
            scores = (
                jnp.concatenate([masked, scores[:, wide:]], axis=1) if lo + wide < 896 else masked
            )
        top = jnp.max(scores, axis=0, keepdims=True) * SCALE2
        if i > 0:
            old = top_ref[:, lo:]
            top = jnp.maximum(old, top)
            factor = jnp.exp2(old - top)
        probs = jnp.exp2(scores * SCALE2 - top)
        total = jnp.sum(probs, axis=0, keepdims=True)
        acc = lax.dot_general(
            rows_of(values, step),
            probs.astype(jnp.bfloat16),
            TN,
            preferred_element_type=jnp.float32,
        )
        if i > 0:
            total += total_ref[:, lo:] * factor
            acc += acc_ref[:, lo:] * factor
        top_ref[:, lo:] = top
        total_ref[:, lo:] = total
        acc_ref[:, lo:] = acc
    out_ref[...] = (acc_ref[...] / total_ref[...]).T.astype(jnp.bfloat16)


def out_kernel(where, resid_ref, own_ref, other_ref, *refs):
    a_refs, b_refs = refs[:8], refs[8:16]
    hid_ref, xs, acc_ref = refs[16:]
    for base, group, swapped in ((0, a_refs, False), (4, b_refs, True)):
        for ref, at, spot in spots_of(where, group, swapped):
            xs[base : base + 4, pl.ds(pl.multiple_of(spot * 16, 16), 16), :] = ref[at]
    for h in range(2):
        acc_ref[h] = resid_ref[h].astype(jnp.float32)
    for i, offset in enumerate((0, -1, 1, -2, 2, -3, 3, 4)):
        z = (where[4] + offset) & 7
        for other, w_ref in enumerate((own_ref, other_ref)):
            x = xs[(z & 3) * 2 + (where[5] ^ other)]
            acc_ref[z >> 2] += lax.dot_general(
                w_ref[i], x, NT, preferred_element_type=jnp.float32
            )
    for h in range(2):
        hid_ref[h] = acc_ref[h].astype(jnp.bfloat16)


def ffn_kernel(swapped, where, gate_ref, up_ref, gain_ref, *refs):
    out_ref, xs = refs[8:]
    squares = jnp.zeros((8, 256), jnp.float32)
    for ref, at, spot in spots_of(where, refs[:8], swapped):
        for h in range(2):
            rows = pl.ds(pl.multiple_of(h * 3584 + spot * 224, 32), 224)
            wide = ref[at, h].astype(jnp.float32)
            xs[rows, :] = (wide * gain_ref[rows, :].astype(jnp.float32)).astype(jnp.bfloat16)
            squares += jnp.sum((wide * wide).reshape(28, 8, 256), axis=0)
    inverse = lax.rsqrt(jnp.sum(squares, axis=0, keepdims=True) / D + 1e-05)
    gate = lax.dot_general(gate_ref[...], xs[...], NN, preferred_element_type=jnp.float32)
    gate *= inverse
    up = lax.dot_general(up_ref[...], xs[...], NN, preferred_element_type=jnp.float32)
    out_ref[...] = (gate / (1.0 + jnp.exp(-gate)) * (up * inverse)).astype(jnp.bfloat16)


SMEM = pl.BlockSpec(memory_space=pltpu.SMEM)
VMEM = pl.BlockSpec(memory_space=pltpu.VMEM)
ANY = pl.BlockSpec(memory_space=pl.ANY)


def call(body, out_shape, scratch, specs, flops, mib=12):
    many = isinstance(out_shape, (tuple, list))
    return pl.pallas_call(
        body,
        out_shape=out_shape,
        in_specs=[SMEM] + specs,
        out_specs=[VMEM] * len(out_shape) if many else VMEM,
        scratch_shapes=scratch,
        compiler_params=pltpu.CompilerParams(vmem_limit_bytes=mib * 1024 * 1024),
        cost_estimate=pl.CostEstimate(flops=flops, bytes_accessed=0, transcendentals=0),
    )


def local(
    queries,
    suffix_kv,
    cache,
    block_list,
    counts,
    out_weight,
    residual,
    norm_gain,
    gate_weight,
    up_weight,
):
    bf16, f32 = jnp.bfloat16, jnp.float32
    place = lax.axis_index("ctx")
    zh, y, x = place // 16, place // 4 % 4, place % 4
    store = lax.axis_index("store")
    where = jnp.stack([zh, y, x, place, zh * 4 + store // 2, store % 2]).astype(jnp.int32)

    with jax.named_scope("prefix"):
        chosen = jnp.take(cache[0], block_list[0], axis=0, mode="clip")
        chosen = chosen.reshape(32, 8, 2 * HD).transpose(1, 0, 2)
        groups = [
            [s * 32 + cidx(h, yy, xx) for h in range(2) for s in range(8)]
            for yy in range(4)
            for xx in range(4)
        ]
        fetched = lax.all_to_all(
            jnp.concatenate([chosen, chosen]),
            ("store", "ctx"),
            split_axis=0,
            concat_axis=0,
            tiled=True,
            axis_index_groups=groups,
        )
        eight = jnp.arange(8, dtype=jnp.int32)
        slot = jnp.arange(32, dtype=jnp.int32)
        ends = jnp.sum(jnp.where(eight[None, :] <= eight[:, None], counts[None, :], 0), axis=1)
        group = jnp.sum((slot[:, None] >= ends[None, :]).astype(jnp.int32), axis=1)
        begin = jnp.sum(jnp.where(eight[None, :] < group[:, None], counts[None, :], 0), axis=1)
        pick = group * 8 + slot - begin
        pick = jnp.concatenate([pick, pick + 64])
        real = jnp.take(fetched.reshape(128, 4, 2 * HD), pick, axis=0, mode="clip")
        real = real.reshape(2, 128, 2 * HD)

    with jax.named_scope("keys"):
        both = jnp.concatenate([suffix_kv[None], swap_h(suffix_kv)[None], real])
        kv_a, kv_b = plane_gather(both[:, :, :HD], both[:, :, HD:])

    with jax.named_scope("queries"):
        gain_part = jnp.broadcast_to(jnp.pad(norm_gain, (0, 288)).reshape(1, 4, HD), (32, 4, HD))
        sent = jnp.concatenate([queries.reshape(32, 4, GQ * HD), gain_part], axis=2)
        sent += nothing(kv_a[2][0, 0, 0, 0])
        came = lax.all_to_all(sent, "ctx", split_axis=0, concat_axis=0, tiled=True)
        q = came[:, :, : GQ * HD].reshape(128 * GQ, HD)
        gain_all = came[:, :, GQ * HD :].reshape(32, 4 * HD)[:, :224].reshape(D, 1)

    with jax.named_scope("weights"):
        *w_seven, low, high = z_gather(out_weight.T)

    with jax.named_scope("order"):
        half = jnp.arange(256, dtype=jnp.int32)
        half = half // 4 % 4 * 128 + half // 16 * 4 + half % 4
        half = jnp.concatenate([half + 64 * zh, half + 64 * (1 - zh)])
        order = (half[:, None] == jnp.arange(512, dtype=jnp.int32)[None, :]).astype(bf16)
        resid = lax.dot_general(
            residual.T, order, NT, preferred_element_type=f32
        ).astype(bf16)
        mine, theirs = resid[:, :256], swap_h(resid[:, 256:])
        resid = jnp.where(zh == 0, jnp.stack([mine, theirs]), jnp.stack([theirs, mine]))

    with jax.named_scope("attend"):
        attended = call(
            attend_kernel,
            jax.ShapeDtypeStruct((896, HD), bf16),
            [
                pltpu.VMEM((16, 4, 128, HD), bf16),
                pltpu.VMEM((16, 4, 128, HD), bf16),
                pltpu.VMEM((HD, 896), f32),
                pltpu.VMEM((1, 896), f32),
                pltpu.VMEM((1, 896), f32),
                pltpu.SemaphoreType.DMA((32,)),
            ],
            [VMEM] + [ANY] * 16,
            flops=20 * 10**9,
            mib=24,
        )(where, q, *kv_a, *kv_b)

    with jax.named_scope("project"):
        w_own = jnp.stack([*w_seven, jnp.concatenate([low, high])]) + nothing(attended[0, 0])
        w_other = swap_core(w_own)
        sent = lax.all_to_all(
            attended.reshape(8, 16, GQ * HD), "store", split_axis=0, concat_axis=0, tiled=True
        )
        att_a, att_b = plane_gather(sent[:4], sent[4:])
        hid = call(
            out_kernel,
            jax.ShapeDtypeStruct((2, 224, 256), bf16),
            [
                pltpu.VMEM((8, 256, GQ * HD), bf16),
                pltpu.VMEM((2, 224, 256), f32),
            ],
            [VMEM] * 19,
            flops=6 * 10**9,
        )(where, resid, w_own, w_other, *att_a, *att_b)

    with jax.named_scope("feed"):
        def ffn(pieces, swapped):
            return call(
                functools.partial(ffn_kernel, swapped),
                jax.ShapeDtypeStruct((320, 256), bf16),
                [pltpu.VMEM((D, 256), bf16)],
                [VMEM] * 11,
                flops=7 * 10**9,
            )(where, gate_weight.T, up_weight.T, gain_all, *pieces)

        other = swap_h(hid)
        near = ffn(gather(hid[None], shift_x, shift_y), False)
        far = ffn(gather(other[None], shift_y, shift_x), True)
        pair = jnp.concatenate(
            [jnp.where(zh == 0, hid[0], hid[1]), jnp.where(zh == 0, other[0], other[1])], axis=1
        )
        hidden_state = jnp.dot(pair, order, preferred_element_type=f32).astype(bf16).T
        both = jnp.concatenate([near, far], axis=1)
        swiglu = jnp.dot(both, order, preferred_element_type=f32).astype(bf16).T
    return (hidden_state, swiglu)


def solution(mesh):
    return jax.shard_map(
        local,
        mesh=mesh,
        in_specs=(
            P("ctx", "store"),
            P("ctx", "store"),
            P("store", None, "ctx", None),
            P("store", None),
            P(),
            P("store", "ctx"),
            P("store", "ctx"),
            P("ctx"),
            P(None, "ctx"),
            P(None, "ctx"),
        ),
        out_specs=(P("store", "ctx"), P("store", "ctx")),
        check_vma=False,
    )
```
